32 devices in a mesh: groups: 2 (over y), ex: 4 (over x, core), par: 4 (over z).
Axes of the slice: x: 2, y: 2, z: 4, core: 2. Of those that a mesh axis runs over, the one named last changes fastest.
Arguments:
- x_in1: bfloat16 [8192, 4096], P(('groups', 'ex'), 'par'), parts along dimension 0, may hold values from -6 to 6
- g_out1: bfloat16 [8192, 11008], P(('groups', 'ex'), 'par'), parts along dimension 0, may hold values from -6 to 6
- x_in2: bfloat16 [8192, 11008], P(('groups', 'ex'), 'par'), parts along dimension 0, may hold values from -6 to 6
- g_out2: bfloat16 [8192, 4096], P(('groups', 'ex'), 'par'), parts along dimension 0, may hold values from -6 to 6
- codebook_d: bfloat16 [16, 128, 64], replicated, may hold values from -0.09375 to 0.09375
- codebook_f: bfloat16 [16, 172, 64], replicated, may hold values from -0.0546875 to 0.0546875
- blocks_d: int32 [2, 32], P(None, 'par'), may hold values from 0 to 15
- blocks_f: int32 [2, 64], P(None, 'par'), may hold values from 0 to 15
- lengths: int32 [8, 16], P(('groups', 'ex')), parts along dimension 0, may hold values from 1 to 256, 1024 in all within a row
- bank: bfloat16 [512, 8192], P('ex', 'par'), may hold values from -0.0078125 to 0.0078125
- query_ids: int32 [1024], replicated, may hold values from 0 to 511
Outputs:
- scores: float32 [128, 1024], P(('groups', 'ex'), 'par'), parts along dimension 0
The draws below stay inside these ranges and needn't reach their ends.
There are 2 independent parts, one for each index of `groups`. The reference program is written for one: setup_inputs(seed, part) draws one part's arguments, and reference() takes and returns one part's arrays. A program takes and returns all parts, laid end to end along the dimension named above; an argument that names none is the same for every part. Nothing has to cross between parts.
Inputs may be any that keep to these rules, and one draw needn't show every extreme that they name: `blocks_d`: every entry names a codebook block. `blocks_f`: every entry names a codebook block. `lengths`: each row sums to 1024; the longest example of each sequence has exactly 256 tokens. `query_ids`: any bank entry, repeats allowed.
All inputs are finite; a program needn't handle non-finite values.
Results may differ from the reference program's by a relative error of at most 0.0051.
Values may be sent and summed in bfloat16 or wider, within the bound.
A program may use at most 64 MiB of HBM per device.

```python
import math
import jax
import jax.numpy as jnp
import numpy as np
from jax import lax

D = 4096
FF = 11008
BW = 128
FF_BLOCKS = 64
D_BLOCKS = 32
FBW = 172
RANK = 64
NTAB = 16
TOK_DEV = 1024
EXD = 16
MOST_LEN = 256
NQ = 1024
SEQS = 4
TOKENS = 4096
EXAMPLES = 64
NBANK = 512


def place_ends(array, key, smallest, largest):
    dims = array.shape
    place = [jax.random.randint(jax.random.fold_in(key, axis), (), 0, dims[axis]) for axis in range(len(dims))]
    array = array.at[tuple(place)].set(smallest)
    longest = dims.index(max(dims))
    place[longest] = (place[longest] + 1) % dims[longest]
    return array.at[tuple(place)].set(largest)


def level_of(own_key, shape, split, low, top_value):
    loudness, own = 1.0, jax.random.fold_in(own_key, 6)
    for dim, parts in split:
        draws = jnp.exp(jax.random.uniform(jax.random.fold_in(own, dim), (parts,), jnp.float32, low / len(split), top_value / len(split)))
        loudness = loudness * jnp.repeat(draws, shape[dim] // parts).reshape([-1 if axis == dim else 1 for axis in range(len(shape))])
    return loudness


def split_up(amount, total, reach, lean):
    loads = [(1 << 20) // math.isqrt(rank ** lean) + 1 for rank in range(2, amount + 1)]
    rest, counts = total - reach - (amount - 1), [1] * (amount - 1)
    while rest > 0:
        candidates = [i for i in range(amount - 1) if counts[i] < reach]
        whole, remaining = sum([loads[i] for i in candidates]), rest
        for i in candidates:
            addition = min(reach - counts[i], max(1, remaining * loads[i] // whole), rest)
            counts[i] = counts[i] + addition
            rest = rest - addition
    return np.array([reach] + counts)


def ragged(rng, amount, total, limit, lean):
    if amount == 2:
        one = jax.random.randint(rng, (), max(1, total - limit), min(limit, total - 1) + 1)
        return jnp.stack([one, total - one])
    sizes = jnp.asarray(split_up(amount, total, limit, lean), jnp.int32)
    couples = (amount - 1) // 2
    source_of, taker = sizes[1:1 + 2 * couples:2], sizes[2:2 + 2 * couples:2]
    slack = jnp.minimum(source_of - 1, limit - taker)
    shifted = jax.random.randint(jax.random.fold_in(rng, 1), (couples,), 0, 1 << 20) % (slack + 1)
    sizes = sizes.at[1:1 + 2 * couples:2].set(source_of - shifted).at[2:2 + 2 * couples:2].set(taker + shifted)
    return sizes[jax.random.permutation(jax.random.fold_in(rng, 2), amount)]


def scatter_about(own_key, dims, width, most, split=(), kind=jnp.bfloat16):
    array = width * jax.random.normal(own_key, dims, jnp.float32)
    if split:
        array = array * level_of(own_key, dims, split, -0.22, 0.18)
    return jnp.clip(array, -most, most).astype(kind)


def setup_inputs(seed: int = 0, part: int = 0) -> dict:
    key_of = jax.random.split(jax.random.key(seed), 12)
    part_keys = jax.random.split(jax.random.fold_in(key_of[11], part), 12)
    x_in1 = scatter_about(part_keys[0], (TOKENS, D), 1.0, 6.0, ((0, 4), (1, 4)))
    g_out1 = scatter_about(part_keys[1], (TOKENS, FF), 1.0, 6.0, ((0, 4), (1, 4)))
    x_in2 = scatter_about(part_keys[2], (TOKENS, FF), 1.0, 6.0, ((0, 4), (1, 4)))
    g_out2 = scatter_about(part_keys[3], (TOKENS, D), 1.0, 6.0, ((0, 4), (1, 4)))
    codebook_d = scatter_about(key_of[4], (NTAB, BW, RANK), D ** -0.5, 0.09375)
    codebook_f = scatter_about(key_of[5], (NTAB, FBW, RANK), FF ** -0.5, 0.0546875)
    blocks_d = place_ends(jax.random.randint(key_of[6], (2, D_BLOCKS), 0, NTAB), jax.random.fold_in(key_of[6], 1), 0, NTAB - 1).astype(jnp.int32)
    blocks_f = place_ends(jax.random.randint(key_of[7], (2, FF_BLOCKS), 0, NTAB), jax.random.fold_in(key_of[7], 1), 0, NTAB - 1).astype(jnp.int32)
    lengths = jax.vmap(lambda own: ragged(own, EXD, TOK_DEV, MOST_LEN, 2))(jax.random.split(part_keys[8], SEQS)).reshape((SEQS, EXD)).astype(jnp.int32)
    bank = scatter_about(key_of[9], (NBANK, 2 * RANK * RANK), (2 * RANK * RANK * TOK_DEV // EXD) ** -0.5, 0.0078125, ((0, 4), (1, 4)))
    query_ids = place_ends(jax.random.randint(key_of[10], (NQ,), 0, NBANK), jax.random.fold_in(key_of[10], 1), 0, NBANK - 1).astype(jnp.int32)
    return {"x_in1": x_in1, "g_out1": g_out1, "x_in2": x_in2, "g_out2": g_out2, "codebook_d": codebook_d, "codebook_f": codebook_f, "blocks_d": blocks_d, "blocks_f": blocks_f, "lengths": lengths, "bank": bank, "query_ids": query_ids}


def codebook_matrix(picks, codebook):
    return codebook[picks].reshape(-1, codebook.shape[2])


def example_grads(block):
    rows_block, lens = block
    ends = jnp.cumsum(lens).astype(jnp.int32)
    starts = ends - lens
    position = jnp.arange(TOK_DEV, dtype=jnp.int32)[:, None]
    member = ((position >= starts[None, :]) & (position < ends[None, :])).astype(jnp.bfloat16)
    pieces = []
    for layer in range(2):
        out_side = rows_block[:, 2 * RANK * layer:2 * RANK * layer + RANK]
        in_side = rows_block[:, 2 * RANK * layer + RANK:2 * RANK * layer + 2 * RANK]
        weighted = (member[:, :, None] * out_side[:, None, :]).reshape(TOK_DEV, EXD * RANK)
        outer = lax.dot_general(weighted, in_side, (((0,), (0,)), ((), ())), preferred_element_type=jnp.float32)
        pieces.append(outer.reshape(EXD, RANK * RANK))
    return jnp.concatenate(pieces, axis=1).astype(jnp.bfloat16)


def reference(x_in1, g_out1, x_in2, g_out2, codebook_d, codebook_f, blocks_d, blocks_f, lengths, bank, query_ids):
    proj_g1 = jnp.dot(g_out1, codebook_matrix(blocks_f[0], codebook_f), preferred_element_type=jnp.float32)
    proj_x1 = jnp.dot(x_in1, codebook_matrix(blocks_d[0], codebook_d), preferred_element_type=jnp.float32)
    proj_g2 = jnp.dot(g_out2, codebook_matrix(blocks_d[1], codebook_d), preferred_element_type=jnp.float32)
    proj_x2 = jnp.dot(x_in2, codebook_matrix(blocks_f[1], codebook_f), preferred_element_type=jnp.float32)
    rows = jnp.concatenate([proj_g1, proj_x1, proj_g2, proj_x2], axis=1).astype(jnp.bfloat16)
    rows = rows.reshape(SEQS, TOK_DEV, 4 * RANK)
    grads = lax.map(example_grads, (rows, lengths)).reshape(EXAMPLES, 2 * RANK * RANK)
    queries = bank[query_ids]
    return jnp.dot(grads, queries.T, preferred_element_type=jnp.float32)
```

```python
import functools

import jax
import jax.numpy as jnp
from jax import lax
from jax.experimental import pallas as pl
from jax.experimental.pallas import tpu as pltpu
from jax.sharding import PartitionSpec as P

MESH = pl.DeviceIdType.MESH
LAYERS = 2
BANK_PIECES = 4


def kernel(
    par_count,
    ex_count,
    chunks,
    x1_ref,
    g1_ref,
    x2_ref,
    g2_ref,
    cbd_ref,
    cbf_ref,
    bd_ref,
    bf_ref,
    len_ref,
    bank_ref,
    qid_ref,
    out_ref,
    wide_s,
    narrow_s,
    tall,
    pw,
    pn,
    stage,
    recv,
    own,
    rows,
    turned,
    weighted,
    outer,
    grads,
    banks,
    onehot,
    part_s,
    part_r,
    in_sem,
    send_sem,
    recv_sem,
    row_send,
    row_recv,
    bank_local,
    bank_send,
    bank_recv,
    fwd_send,
    fwd_recv,
    sc_send,
    sc_recv,
):
    rank = cbd_ref.shape[2]
    group = par_count // LAYERS
    per = chunks // group
    size = wide_s.shape[2]
    width = rank // group
    count_ex = len_ref.shape[1]
    me = lax.axis_index("par")
    ex = lax.axis_index("ex")
    layer = me // group
    place = lax.rem(me, group)
    core = lax.rem(ex, 2)
    sibling = ex + 1 - 2 * core
    piece_rows = banks.shape[2]

    def order(step):
        far = step < chunks
        inner = lax.rem(step, chunks)
        l = jnp.where(far, 1 - layer, layer)
        shift = jnp.where(far, place * per, (place + 1) * per)
        return l, lax.rem(inner + shift, chunks)

    wides = (g1_ref, x2_ref)
    narrows = (x1_ref, g2_ref)

    def fetch(l, c):
        span = pl.ds(pl.multiple_of(c * size, size), size)
        pltpu.make_async_copy(wides[l].at[span, :], wide_s.at[l, c], in_sem.at[l, c, 0]).start()
        pltpu.make_async_copy(narrows[l].at[span, :], narrow_s.at[l, c], in_sem.at[l, c, 1]).start()

    for mine in range(LAYERS):
        @pl.when(layer == mine)
        def _(mine=mine):
            for step in range(2 * chunks):
                fetch((1 - mine) if step < chunks else mine, order(step)[1])

    local_bank = []
    for i in range(BANK_PIECES):
        span = pl.ds(i * piece_rows, piece_rows)
        copy = pltpu.make_async_copy(bank_ref.at[span, :], banks.at[ex, i], bank_local.at[i])
        copy.start()
        local_bank.append(copy)

    barrier = pltpu.get_barrier_semaphore()
    for k in range(1, par_count):
        pl.semaphore_signal(barrier, inc=1, device_id={"par": lax.rem(me + k, par_count)}, device_id_type=MESH)
    for k in range(1, ex_count // 2):
        pl.semaphore_signal(barrier, inc=1, device_id={"ex": lax.rem(ex + 2 * k, ex_count)}, device_id_type=MESH)
    pl.semaphore_signal(barrier, inc=1, device_id={"ex": sibling}, device_id_type=MESH)

    depth = cbf_ref.shape[1]
    high = tall.shape[0]
    for l in range(LAYERS):
        fill = jnp.zeros((depth, rank), jnp.float32)
        for b in range(bf_ref.shape[1]):
            block = cbf_ref[bf_ref[l, b]].astype(jnp.float32)
            both = [block, fill] if l == 0 else [fill, block]
            tall[b * depth:(b + 1) * depth, :] = jnp.concatenate(both, axis=1)
        pw[l] = tall[...].astype(jnp.bfloat16)
        deep = cbd_ref.shape[1]
        fill = jnp.zeros((deep, rank), jnp.float32)
        for b in range(bd_ref.shape[1]):
            block = cbd_ref[bd_ref[l, b]].astype(jnp.float32)
            both = [fill, block] if l == 0 else [block, fill]
            pn[l, b * deep:(b + 1) * deep, :] = jnp.concatenate(both, axis=1).astype(jnp.bfloat16)

    pl.semaphore_wait(barrier, par_count - 1 + ex_count // 2)

    for i in range(BANK_PIECES):
        span = pl.ds(i * piece_rows, piece_rows)
        for k in range(1, ex_count // 2):
            pltpu.make_async_remote_copy(
                bank_ref.at[span, :], banks.at[ex, i], bank_send.at[k, i], bank_recv.at[ex, i],
                device_id={"ex": lax.rem(ex + 2 * k, ex_count)}, device_id_type=MESH,
            ).start()
    for i in range(BANK_PIECES):
        span = pl.ds(i * piece_rows, piece_rows)
        pltpu.make_async_remote_copy(
            bank_ref.at[span, :], banks.at[ex, i], bank_send.at[0, i], bank_recv.at[ex, i],
            device_id={"ex": sibling}, device_id_type=MESH,
        ).start()

    def project(l, c):
        span = pl.ds(0, size)
        pltpu.make_async_copy(g1_ref.at[span, :], wide_s.at[l, c], in_sem.at[l, c, 0]).wait()
        pltpu.make_async_copy(x1_ref.at[span, :], narrow_s.at[l, c], in_sem.at[l, c, 1]).wait()
        return jnp.dot(wide_s[l, c], pw[l], preferred_element_type=jnp.float32) + jnp.dot(
            narrow_s[l, c], pn[l], preferred_element_type=jnp.float32
        )

    def partial_copy(step, l, c):
        return pltpu.make_async_remote_copy(
            stage.at[step], recv.at[me, lax.rem(c, per)], send_sem.at[step], recv_sem.at[me, lax.rem(c, per)],
            device_id={"par": l * group + c // per}, device_id_type=MESH,
        )

    sent = 2 * chunks - per

    def send_step(step, carry):
        l, c = order(step)
        stage[step] = project(l, c).astype(jnp.bfloat16)
        partial_copy(step, l, c).start()
        return carry

    lax.fori_loop(0, sent, send_step, 0)

    def keep_step(j, carry):
        own[j] = project(layer, place * per + j)
        return carry

    lax.fori_loop(0, per, keep_step, 0)

    entry = lax.broadcasted_iota(jnp.int32, onehot.shape, 0)
    onehot[...] = (entry == qid_ref[...]).astype(jnp.float32).astype(jnp.bfloat16)
    lane = lax.broadcasted_iota(jnp.int32, (count_ex, size), 1)
    which = lax.broadcasted_iota(jnp.int32, (count_ex, size), 0)
    starts = jnp.zeros((count_ex, size), jnp.int32)
    ends = jnp.zeros((count_ex, size), jnp.int32)
    total = jnp.int32(0)
    for e in range(count_ex):
        starts = jnp.where(which == e, total, starts)
        total = total + len_ref[0, e]
        ends = jnp.where(which == e, total, ends)
    outer[...] = jnp.zeros_like(outer)

    def bank_forward(i):
        for k in range(1, ex_count // 2):
            source = lax.rem(ex + 2 * k, ex_count)
            pltpu.make_async_remote_copy(
                banks.at[source, i], banks.at[source, i], bank_send.at[k, i], bank_recv.at[source, i],
                device_id={"ex": source}, device_id_type=MESH,
            ).wait_recv()
            pltpu.make_async_remote_copy(
                banks.at[source, i], banks.at[source, i], fwd_send.at[k, i], fwd_recv.at[source, i],
                device_id={"ex": sibling}, device_id_type=MESH,
            ).start()

    def add_outer(c):
        held = rows[c]
        turned[...] = held.astype(jnp.float32).T
        token = lane + c * size
        member = ((token >= starts) & (token < ends)).astype(jnp.float32)
        slab = turned[pl.ds(pl.multiple_of(place * width, width), width), :]
        for a in range(width):
            weighted[a * count_ex:(a + 1) * count_ex, :] = (member * slab[a:a + 1, :]).astype(jnp.bfloat16)
        outer[...] += jnp.dot(weighted[...], held, preferred_element_type=jnp.float32)

    def row_copy(k, j):
        c = place * per + j
        return pltpu.make_async_remote_copy(
            rows.at[c], rows.at[c], row_send.at[k, j], row_recv.at[c],
            device_id={"par": layer * group + lax.rem(place + k, group)}, device_id_type=MESH,
        )

    done = 0
    for j in range(per):
        acc = own[j]
        for k in range(1, par_count):
            source = lax.rem(me + k, par_count)
            pltpu.make_async_remote_copy(
                stage.at[0], recv.at[source, j], send_sem.at[0], recv_sem.at[source, j],
                device_id={"par": source}, device_id_type=MESH,
            ).wait_recv()
            acc = acc + recv[source, j].astype(jnp.float32)
        c = place * per + j
        rows[c] = acc.astype(jnp.bfloat16)
        for k in range(1, group):
            row_copy(k, j).start()
        goal = BANK_PIECES * (j + 1) // per
        for i in range(done, goal):
            bank_forward(i)
        done = goal
        add_outer(c)
    for k in range(1, group):
        for j in range(per):
            c = lax.rem(place + k, group) * per + j
            pltpu.make_async_remote_copy(
                rows.at[c], rows.at[c], row_send.at[k, j], row_recv.at[c],
                device_id={"par": layer * group + lax.rem(place + k, group)}, device_id_type=MESH,
            ).wait_recv()
            add_outer(c)

    upper = lax.broadcasted_iota(jnp.int32, (count_ex, 2 * rank), 1) >= rank
    rolled = pltpu.roll(outer[...], rank, 1)
    for pair in range(width // 2):
        even = rolled[2 * pair * count_ex:(2 * pair + 1) * count_ex, :]
        odd = outer[(2 * pair + 1) * count_ex:(2 * pair + 2) * count_ex, :]
        grads[:, 2 * rank * pair:2 * rank * (pair + 1)] = jnp.where(upper, odd, even).astype(jnp.bfloat16)

    for copy in local_bank:
        copy.wait()
    for i in range(BANK_PIECES):
        pltpu.make_async_remote_copy(
            banks.at[sibling, i], banks.at[sibling, i], bank_send.at[0, i], bank_recv.at[sibling, i],
            device_id={"ex": sibling}, device_id_type=MESH,
        ).wait_recv()
        for k in range(1, ex_count // 2):
            source = lax.rem(sibling + 2 * k, ex_count)
            pltpu.make_async_remote_copy(
                banks.at[source, i], banks.at[source, i], fwd_send.at[k, i], fwd_recv.at[source, i],
                device_id={"ex": sibling}, device_id_type=MESH,
            ).wait_recv()

    every = banks[...].reshape(onehot.shape[0], grads.shape[1])
    against = lax.dot_general(grads[...], every, (((1,), (1,)), ((), ())), preferred_element_type=jnp.float32)
    high_part = against.astype(jnp.bfloat16)
    low_part = (against - high_part.astype(jnp.float32)).astype(jnp.bfloat16)
    both = jnp.concatenate([high_part, low_part], axis=0)
    picked = jnp.dot(both, onehot[...], preferred_element_type=jnp.float32)
    picked = picked[:count_ex] + picked[count_ex:]
    share = part_s.shape[2]
    for d in range(par_count):
        part_s[d] = picked[:, d * share:(d + 1) * share]
    for k in range(1, par_count):
        target = lax.rem(me + k, par_count)
        pltpu.make_async_remote_copy(
            part_s.at[target], part_r.at[me], sc_send.at[k], sc_recv.at[me],
            device_id={"par": target}, device_id_type=MESH,
        ).start()
    result = part_s[me]
    for k in range(1, par_count):
        source = lax.rem(me + k, par_count)
        pltpu.make_async_remote_copy(
            part_s.at[source], part_r.at[source], sc_send.at[k], sc_recv.at[source],
            device_id={"par": source}, device_id_type=MESH,
        ).wait_recv()
        result = result + part_r[source]
    out_ref[...] = result

    def sent_step(step, carry):
        l, c = order(step)
        partial_copy(step, l, c).wait_send()
        return carry

    lax.fori_loop(0, sent, sent_step, 0)
    for k in range(1, group):
        for j in range(per):
            row_copy(k, j).wait_send()
    for i in range(BANK_PIECES):
        span = pl.ds(i * piece_rows, piece_rows)
        for k in range(ex_count // 2):
            pltpu.make_async_remote_copy(
                bank_ref.at[span, :], banks.at[ex, i], bank_send.at[k, i], bank_recv.at[ex, i],
                device_id={"ex": sibling}, device_id_type=MESH,
            ).wait_send()
        for k in range(1, ex_count // 2):
            source = lax.rem(ex + 2 * k, ex_count)
            pltpu.make_async_remote_copy(
                banks.at[source, i], banks.at[source, i], fwd_send.at[k, i], fwd_recv.at[source, i],
                device_id={"ex": sibling}, device_id_type=MESH,
            ).wait_send()
    for k in range(1, par_count):
        target = lax.rem(me + k, par_count)
        pltpu.make_async_remote_copy(
            part_s.at[target], part_r.at[me], sc_send.at[k], sc_recv.at[me],
            device_id={"par": target}, device_id_type=MESH,
        ).wait_send()


def on_device(x_in1, g_out1, x_in2, g_out2, codebook_d, codebook_f, blocks_d, blocks_f, lengths, bank, query_ids):
    par_count = lax.axis_size("par")
    ex_count = lax.axis_size("ex")
    tokens, slim = x_in1.shape
    broad = g_out1.shape[1]
    rank = codebook_d.shape[2]
    group = par_count // LAYERS
    chunks = group * max(1, 4 // group)
    per = chunks // group
    size = tokens // chunks
    count_ex = lengths.shape[1]
    width = rank // group
    entries, dims = bank.shape
    queries = query_ids.shape[0]
    share = queries // par_count
    half = ex_count // 2
    bf16, f32 = jnp.bfloat16, jnp.float32
    dma = pltpu.SemaphoreType.DMA
    hbm = pl.BlockSpec(memory_space=pl.ANY)
    vmem = pl.BlockSpec(memory_space=pltpu.VMEM)
    smem = pl.BlockSpec(memory_space=pltpu.SMEM)
    return pl.pallas_call(
        functools.partial(kernel, par_count, ex_count, chunks),
        out_shape=jax.ShapeDtypeStruct((count_ex, share), f32),
        in_specs=[hbm, hbm, hbm, hbm, vmem, vmem, smem, smem, smem, hbm, vmem],
        out_specs=vmem,
        scratch_shapes=[
            pltpu.VMEM((LAYERS, chunks, size, broad), bf16),
            pltpu.VMEM((LAYERS, chunks, size, slim), bf16),
            pltpu.VMEM((broad, 2 * rank), f32),
            pltpu.VMEM((LAYERS, broad, 2 * rank), bf16),
            pltpu.VMEM((LAYERS, slim, 2 * rank), bf16),
            pltpu.VMEM((2 * chunks - per, size, 2 * rank), bf16),
            pltpu.VMEM((par_count, per, size, 2 * rank), bf16),
            pltpu.VMEM((per, size, 2 * rank), f32),
            pltpu.VMEM((chunks, size, 2 * rank), bf16),
            pltpu.VMEM((2 * rank, size), f32),
            pltpu.VMEM((width * count_ex, size), bf16),
            pltpu.VMEM((width * count_ex, 2 * rank), f32),
            pltpu.VMEM((count_ex, dims), bf16),
            pltpu.VMEM((ex_count, BANK_PIECES, entries // BANK_PIECES, dims), bf16),
            pltpu.VMEM((ex_count * entries, queries), bf16),
            pltpu.VMEM((par_count, count_ex, share), f32),
            pltpu.VMEM((par_count, count_ex, share), f32),
            dma((LAYERS, chunks, 2)),
            dma((2 * chunks - per,)),
            dma((par_count, per)),
            dma((group, per)),
            dma((chunks,)),
            dma((BANK_PIECES,)),
            dma((half, BANK_PIECES)),
            dma((ex_count, BANK_PIECES)),
            dma((half, BANK_PIECES)),
            dma((ex_count, BANK_PIECES)),
            dma((par_count,)),
            dma((par_count,)),
        ],
        compiler_params=pltpu.CompilerParams(
            collective_id=0, has_side_effects=True, vmem_limit_bytes=56 * 1024 * 1024
        ),
    )(
        x_in1, g_out1, x_in2, g_out2, codebook_d, codebook_f, blocks_d, blocks_f, lengths, bank,
        query_ids.reshape(1, queries),
    )


def solution(mesh):
    return jax.shard_map(
        on_device,
        mesh=mesh,
        in_specs=(
            P(("groups", "ex"), "par"),
            P(("groups", "ex"), "par"),
            P(("groups", "ex"), "par"),
            P(("groups", "ex"), "par"),
            P(),
            P(),
            P(None, "par"),
            P(None, "par"),
            P(("groups", "ex"), None),
            P("ex", "par"),
            P(),
        ),
        out_specs=P(("groups", "ex"), "par"),
        check_vma=False,
    )
```

```python
import functools

import jax
import jax.numpy as jnp
from jax import lax
from jax.experimental import pallas as pl
from jax.experimental.pallas import tpu as pltpu
from jax.sharding import PartitionSpec as P

MESH = pl.DeviceIdType.MESH
LAYERS = 2
BANK_PIECES = 4


def kernel(
    par_count,
    ex_count,
    chunks,
    x1_ref,
    g1_ref,
    x2_ref,
    g2_ref,
    cbd_ref,
    cbf_ref,
    bd_ref,
    bf_ref,
    len_ref,
    bank_ref,
    qid_ref,
    out_ref,
    wide_s,
    narrow_s,
    tall,
    pw,
    pn,
    stage,
    recv,
    own,
    rows,
    twice,
    weighted,
    outer,
    grads,
    banks,
    onehot,
    part_s,
    part_r,
    in_sem,
    send_sem,
    recv_sem,
    row_send,
    row_recv,
    bank_local,
    bank_send,
    bank_recv,
    fwd_send,
    fwd_recv,
    sc_send,
    sc_recv,
):
    rank = cbd_ref.shape[1]
    group = par_count // LAYERS
    per = chunks // group
    size = wide_s.shape[3]
    width = rank // group
    count_ex = len_ref.shape[1]
    me = lax.axis_index("par")
    ex = lax.axis_index("ex")
    layer = me // group
    place = lax.rem(me, group)
    core = lax.rem(ex, 2)
    sibling = ex + 1 - 2 * core
    piece_rows = banks.shape[2]

    def order(step):
        far = step < chunks
        inner = lax.rem(step, chunks)
        l = jnp.where(far, 1 - layer, layer)
        shift = jnp.where(far, place * per, (place + 1) * per)
        return l, lax.rem(inner + shift, chunks)

    wides = (g1_ref, x2_ref)
    narrows = (x1_ref, g2_ref)

    def fetch(l, c):
        span = pl.ds(pl.multiple_of(c * size, size), size)
        pltpu.make_async_copy(wides[l].at[:, span], wide_s.at[l, c], in_sem.at[l, c, 0]).start()
        pltpu.make_async_copy(narrows[l].at[span, :], narrow_s.at[l, c], in_sem.at[l, c, 1]).start()

    for mine in range(LAYERS):
        @pl.when(layer == mine)
        def _(mine=mine):
            for step in range(2 * chunks):
                fetch((1 - mine) if step < chunks else mine, order(step)[1])

    local_bank = []
    for i in range(BANK_PIECES):
        span = pl.ds(i * piece_rows, piece_rows)
        copy = pltpu.make_async_copy(bank_ref.at[span, :], banks.at[ex, i], bank_local.at[i])
        copy.start()
        local_bank.append(copy)

    barrier = pltpu.get_barrier_semaphore()
    for k in range(1, par_count):
        pl.semaphore_signal(barrier, inc=1, device_id={"par": lax.rem(me + k, par_count)}, device_id_type=MESH)
    for k in range(1, ex_count // 2):
        pl.semaphore_signal(barrier, inc=1, device_id={"ex": lax.rem(ex + 2 * k, ex_count)}, device_id_type=MESH)
    pl.semaphore_signal(barrier, inc=1, device_id={"ex": sibling}, device_id_type=MESH)

    depth, deep = cbf_ref.shape[2], cbd_ref.shape[2]
    for l in range(LAYERS):
        for b in range(bf_ref.shape[1]):
            tall[:, b * depth:(b + 1) * depth] = cbf_ref[bf_ref[l, b]].astype(jnp.float32)
        pw[l] = tall[...].astype(jnp.bfloat16)
        for b in range(bd_ref.shape[1]):
            pn[l, :, b * deep:(b + 1) * deep] = cbd_ref[bd_ref[l, b]]

    pl.semaphore_wait(barrier, par_count - 1 + ex_count // 2)

    for i in range(BANK_PIECES):
        span = pl.ds(i * piece_rows, piece_rows)
        for k in range(1, ex_count // 2):
            pltpu.make_async_remote_copy(
                bank_ref.at[span, :], banks.at[ex, i], bank_send.at[k, i], bank_recv.at[ex, i],
                device_id={"ex": lax.rem(ex + 2 * k, ex_count)}, device_id_type=MESH,
            ).start()
    for i in range(BANK_PIECES):
        span = pl.ds(i * piece_rows, piece_rows)
        pltpu.make_async_remote_copy(
            bank_ref.at[span, :], banks.at[ex, i], bank_send.at[0, i], bank_recv.at[ex, i],
            device_id={"ex": sibling}, device_id_type=MESH,
        ).start()

    def project(l, c):
        span = pl.ds(0, size)
        pltpu.make_async_copy(g1_ref.at[:, span], wide_s.at[l, c], in_sem.at[l, c, 0]).wait()
        pltpu.make_async_copy(x1_ref.at[span, :], narrow_s.at[l, c], in_sem.at[l, c, 1]).wait()
        first = jnp.dot(pw[l], wide_s[l, c], preferred_element_type=jnp.float32)
        second = lax.dot_general(
            pn[l], narrow_s[l, c], (((1,), (1,)), ((), ())), preferred_element_type=jnp.float32
        )
        return first, second

    def partial_copy(step, l, c):
        return pltpu.make_async_remote_copy(
            stage.at[step], recv.at[me, lax.rem(c, per)], send_sem.at[step], recv_sem.at[me, lax.rem(c, per)],
            device_id={"par": l * group + c // per}, device_id_type=MESH,
        )

    sent = 2 * chunks - per

    def send_step(step, carry):
        l, c = order(step)
        first, second = project(l, c)
        stage[step, :rank, :] = first.astype(jnp.bfloat16)
        stage[step, rank:, :] = second.astype(jnp.bfloat16)
        partial_copy(step, l, c).start()
        return carry

    lax.fori_loop(0, sent, send_step, 0)

    def keep_step(j, carry):
        first, second = project(layer, place * per + j)
        own[j, :rank, :] = first
        own[j, rank:, :] = second
        return carry

    lax.fori_loop(0, per, keep_step, 0)

    entry = lax.broadcasted_iota(jnp.int32, onehot.shape, 0)
    onehot[...] = (entry == qid_ref[...]).astype(jnp.float32).astype(jnp.bfloat16)
    lane = lax.broadcasted_iota(jnp.int32, (count_ex, size), 1)
    which = lax.broadcasted_iota(jnp.int32, (count_ex, size), 0)
    starts = jnp.zeros((count_ex, size), jnp.int32)
    ends = jnp.zeros((count_ex, size), jnp.int32)
    total = jnp.int32(0)
    for e in range(count_ex):
        starts = jnp.where(which == e, total, starts)
        total = total + len_ref[0, e]
        ends = jnp.where(which == e, total, ends)
    outer[...] = jnp.zeros_like(outer)

    def bank_forward(i):
        for k in range(1, ex_count // 2):
            source = lax.rem(ex + 2 * k, ex_count)
            pltpu.make_async_remote_copy(
                banks.at[source, i], banks.at[source, i], bank_send.at[k, i], bank_recv.at[source, i],
                device_id={"ex": source}, device_id_type=MESH,
            ).wait_recv()
            pltpu.make_async_remote_copy(
                banks.at[source, i], banks.at[source, i], fwd_send.at[k, i], fwd_recv.at[source, i],
                device_id={"ex": sibling}, device_id_type=MESH,
            ).start()

    def add_outer(c):
        token = lane + c * size
        member = ((token >= starts) & (token < ends)).astype(jnp.float32)
        slab = rows[c, pl.ds(pl.multiple_of(layer * rank + place * width, width), width), :].astype(jnp.float32)
        for a in range(width):
            weighted[a * count_ex:(a + 1) * count_ex, :] = (member * slab[a:a + 1, :]).astype(jnp.bfloat16)
        inside = rows[c, pl.ds(pl.multiple_of((1 - layer) * rank, rank), rank), :]
        twice[:rank, :] = inside
        twice[rank:, :] = inside
        outer[...] += lax.dot_general(
            weighted[...], twice[...], (((1,), (1,)), ((), ())), preferred_element_type=jnp.float32
        )

    def row_copy(k, j):
        c = place * per + j
        return pltpu.make_async_remote_copy(
            rows.at[c], rows.at[c], row_send.at[k, j], row_recv.at[c],
            device_id={"par": layer * group + lax.rem(place + k, group)}, device_id_type=MESH,
        )

    done = 0
    for j in range(per):
        acc = own[j]
        for k in range(1, par_count):
            source = lax.rem(me + k, par_count)
            pltpu.make_async_remote_copy(
                stage.at[0], recv.at[source, j], send_sem.at[0], recv_sem.at[source, j],
                device_id={"par": source}, device_id_type=MESH,
            ).wait_recv()
            acc = acc + recv[source, j].astype(jnp.float32)
        c = place * per + j
        rows[c] = acc.astype(jnp.bfloat16)
        for k in range(1, group):
            row_copy(k, j).start()
        goal = BANK_PIECES * (j + 1) // per
        for i in range(done, goal):
            bank_forward(i)
        done = goal
        add_outer(c)
    for k in range(1, group):
        for j in range(per):
            c = lax.rem(place + k, group) * per + j
            pltpu.make_async_remote_copy(
                rows.at[c], rows.at[c], row_send.at[k, j], row_recv.at[c],
                device_id={"par": layer * group + lax.rem(place + k, group)}, device_id_type=MESH,
            ).wait_recv()
            add_outer(c)

    upper = lax.broadcasted_iota(jnp.int32, (count_ex, 2 * rank), 1) >= rank
    for pair in range(width // 2):
        even = outer[2 * pair * count_ex:(2 * pair + 1) * count_ex, :]
        odd = outer[(2 * pair + 1) * count_ex:(2 * pair + 2) * count_ex, :]
        grads[:, 2 * rank * pair:2 * rank * (pair + 1)] = jnp.where(upper, odd, even).astype(jnp.bfloat16)

    for copy in local_bank:
        copy.wait()
    for i in range(BANK_PIECES):
        pltpu.make_async_remote_copy(
            banks.at[sibling, i], banks.at[sibling, i], bank_send.at[0, i], bank_recv.at[sibling, i],
            device_id={"ex": sibling}, device_id_type=MESH,
        ).wait_recv()
        for k in range(1, ex_count // 2):
            source = lax.rem(sibling + 2 * k, ex_count)
            pltpu.make_async_remote_copy(
                banks.at[source, i], banks.at[source, i], fwd_send.at[k, i], fwd_recv.at[source, i],
                device_id={"ex": sibling}, device_id_type=MESH,
            ).wait_recv()

    every = banks[...].reshape(onehot.shape[0], grads.shape[1])
    against = lax.dot_general(grads[...], every, (((1,), (1,)), ((), ())), preferred_element_type=jnp.float32)
    high_part = against.astype(jnp.bfloat16)
    low_part = (against - high_part.astype(jnp.float32)).astype(jnp.bfloat16)
    both = jnp.concatenate([high_part, low_part], axis=0)
    picked = jnp.dot(both, onehot[...], preferred_element_type=jnp.float32)
    picked = picked[:count_ex] + picked[count_ex:]
    share = part_s.shape[2]
    for d in range(par_count):
        part_s[d] = picked[:, d * share:(d + 1) * share]
    for k in range(1, par_count):
        target = lax.rem(me + k, par_count)
        pltpu.make_async_remote_copy(
            part_s.at[target], part_r.at[me], sc_send.at[k], sc_recv.at[me],
            device_id={"par": target}, device_id_type=MESH,
        ).start()
    result = part_s[me]
    for k in range(1, par_count):
        source = lax.rem(me + k, par_count)
        pltpu.make_async_remote_copy(
            part_s.at[source], part_r.at[source], sc_send.at[k], sc_recv.at[source],
            device_id={"par": source}, device_id_type=MESH,
        ).wait_recv()
        result = result + part_r[source]
    out_ref[...] = result

    def sent_step(step, carry):
        l, c = order(step)
        partial_copy(step, l, c).wait_send()
        return carry

    lax.fori_loop(0, sent, sent_step, 0)
    for k in range(1, group):
        for j in range(per):
            row_copy(k, j).wait_send()
    for i in range(BANK_PIECES):
        span = pl.ds(i * piece_rows, piece_rows)
        for k in range(ex_count // 2):
            pltpu.make_async_remote_copy(
                bank_ref.at[span, :], banks.at[ex, i], bank_send.at[k, i], bank_recv.at[ex, i],
                device_id={"ex": sibling}, device_id_type=MESH,
            ).wait_send()
        for k in range(1, ex_count // 2):
            source = lax.rem(ex + 2 * k, ex_count)
            pltpu.make_async_remote_copy(
                banks.at[source, i], banks.at[source, i], fwd_send.at[k, i], fwd_recv.at[source, i],
                device_id={"ex": sibling}, device_id_type=MESH,
            ).wait_send()
    for k in range(1, par_count):
        target = lax.rem(me + k, par_count)
        pltpu.make_async_remote_copy(
            part_s.at[target], part_r.at[me], sc_send.at[k], sc_recv.at[me],
            device_id={"par": target}, device_id_type=MESH,
        ).wait_send()


def on_device(x_in1, g_out1, x_in2, g_out2, codebook_d, codebook_f, blocks_d, blocks_f, lengths, bank, query_ids):
    par_count = lax.axis_size("par")
    ex_count = lax.axis_size("ex")
    tokens, slim = x_in1.shape
    broad = g_out1.shape[1]
    rank = codebook_d.shape[2]
    group = par_count // LAYERS
    chunks = group * max(1, 4 // group)
    per = chunks // group
    size = tokens // chunks
    count_ex = lengths.shape[1]
    width = rank // group
    entries, dims = bank.shape
    queries = query_ids.shape[0]
    share = queries // par_count
    half = ex_count // 2
    bf16, f32 = jnp.bfloat16, jnp.float32
    dma = pltpu.SemaphoreType.DMA
    hbm = pl.BlockSpec(memory_space=pl.ANY)
    vmem = pl.BlockSpec(memory_space=pltpu.VMEM)
    smem = pl.BlockSpec(memory_space=pltpu.SMEM)
    return pl.pallas_call(
        functools.partial(kernel, par_count, ex_count, chunks),
        out_shape=jax.ShapeDtypeStruct((count_ex, share), f32),
        in_specs=[hbm, hbm, hbm, hbm, vmem, vmem, smem, smem, smem, hbm, vmem],
        out_specs=vmem,
        scratch_shapes=[
            pltpu.VMEM((LAYERS, chunks, broad, size), bf16),
            pltpu.VMEM((LAYERS, chunks, size, slim), bf16),
            pltpu.VMEM((rank, broad), f32),
            pltpu.VMEM((LAYERS, rank, broad), bf16),
            pltpu.VMEM((LAYERS, rank, slim), bf16),
            pltpu.VMEM((2 * chunks - per, 2 * rank, size), bf16),
            pltpu.VMEM((par_count, per, 2 * rank, size), bf16),
            pltpu.VMEM((per, 2 * rank, size), f32),
            pltpu.VMEM((chunks, 2 * rank, size), bf16),
            pltpu.VMEM((2 * rank, size), bf16),
            pltpu.VMEM((width * count_ex, size), bf16),
            pltpu.VMEM((width * count_ex, 2 * rank), f32),
            pltpu.VMEM((count_ex, dims), bf16),
            pltpu.VMEM((ex_count, BANK_PIECES, entries // BANK_PIECES, dims), bf16),
            pltpu.VMEM((ex_count * entries, queries), bf16),
            pltpu.VMEM((par_count, count_ex, share), f32),
            pltpu.VMEM((par_count, count_ex, share), f32),
            dma((LAYERS, chunks, 2)),
            dma((2 * chunks - per,)),
            dma((par_count, per)),
            dma((group, per)),
            dma((chunks,)),
            dma((BANK_PIECES,)),
            dma((half, BANK_PIECES)),
            dma((ex_count, BANK_PIECES)),
            dma((half, BANK_PIECES)),
            dma((ex_count, BANK_PIECES)),
            dma((par_count,)),
            dma((par_count,)),
        ],
        compiler_params=pltpu.CompilerParams(
            collective_id=0, has_side_effects=True, vmem_limit_bytes=56 * 1024 * 1024
        ),
    )(
        x_in1, g_out1.T, x_in2.T, g_out2, codebook_d.transpose(0, 2, 1), codebook_f.transpose(0, 2, 1),
        blocks_d, blocks_f, lengths, bank,
        query_ids.reshape(1, queries),
    )


def solution(mesh):
    return jax.shard_map(
        on_device,
        mesh=mesh,
        in_specs=(
            P(("groups", "ex"), "par"),
            P(("groups", "ex"), "par"),
            P(("groups", "ex"), "par"),
            P(("groups", "ex"), "par"),
            P(),
            P(),
            P(None, "par"),
            P(None, "par"),
            P(("groups", "ex"), None),
            P("ex", "par"),
            P(),
        ),
        out_specs=P(("groups", "ex"), "par"),
        check_vma=False,
    )
```

```python
import functools

import jax
import jax.numpy as jnp
from jax import lax
from jax.experimental import pallas as pl
from jax.experimental.pallas import tpu as pltpu
from jax.sharding import PartitionSpec as P

MESH = pl.DeviceIdType.MESH
LAYERS = 2
BANK_PIECES = 4


def kernel(
    par_count,
    ex_count,
    chunks,
    x1_ref,
    g1_ref,
    x2_ref,
    g2_ref,
    cbd_ref,
    cbf_ref,
    bd_ref,
    bf_ref,
    len_ref,
    bank_ref,
    qid_ref,
    out_ref,
    wide_s,
    narrow_s,
    tall,
    pw,
    pn,
    stage,
    recv,
    own,
    rows,
    twice,
    weighted,
    outer,
    grads,
    banks,
    onehot,
    part_s,
    part_r,
    in_sem,
    send_sem,
    recv_sem,
    row_send,
    row_recv,
    bank_local,
    bank_send,
    bank_recv,
    fwd_send,
    fwd_recv,
    sc_send,
    sc_recv,
):
    rank = cbd_ref.shape[1]
    group = par_count // LAYERS
    per = chunks // group
    size = wide_s.shape[3]
    width = rank // group
    count_ex = len_ref.shape[1]
    me = lax.axis_index("par")
    ex = lax.axis_index("ex")
    layer = me // group
    place = lax.rem(me, group)
    core = lax.rem(ex, 2)
    sibling = ex + 1 - 2 * core
    piece_rows = banks.shape[2]

    def order(step):
        far = step < chunks
        inner = lax.rem(step, chunks)
        l = jnp.where(far, 1 - layer, layer)
        spread = lax.rem(inner + place, group) * per + inner // group
        return l, jnp.where(far, spread, lax.rem(inner + (place + 1) * per, chunks))

    wides = (g1_ref, x2_ref)
    narrows = (x1_ref, g2_ref)

    def fetch(l, c):
        span = pl.ds(pl.multiple_of(c * size, size), size)
        pltpu.make_async_copy(wides[l].at[:, span], wide_s.at[l, c], in_sem.at[l, c, 0]).start()
        pltpu.make_async_copy(narrows[l].at[span, :], narrow_s.at[l, c], in_sem.at[l, c, 1]).start()

    for mine in range(LAYERS):
        @pl.when(layer == mine)
        def _(mine=mine):
            for step in range(2 * chunks):
                fetch((1 - mine) if step < chunks else mine, order(step)[1])

    local_bank = []
    for i in range(BANK_PIECES):
        span = pl.ds(i * piece_rows, piece_rows)
        copy = pltpu.make_async_copy(bank_ref.at[span, :], banks.at[ex, i], bank_local.at[i])
        copy.start()
        local_bank.append(copy)

    barrier = pltpu.get_barrier_semaphore()
    for k in range(1, par_count):
        pl.semaphore_signal(barrier, inc=1, device_id={"par": lax.rem(me + k, par_count)}, device_id_type=MESH)
    for k in range(1, ex_count // 2):
        pl.semaphore_signal(barrier, inc=1, device_id={"ex": lax.rem(ex + 2 * k, ex_count)}, device_id_type=MESH)
    pl.semaphore_signal(barrier, inc=1, device_id={"ex": sibling}, device_id_type=MESH)

    depth, deep = cbf_ref.shape[2], cbd_ref.shape[2]
    for l in range(LAYERS):
        for b in range(bf_ref.shape[1]):
            tall[:, b * depth:(b + 1) * depth] = cbf_ref[bf_ref[l, b]].astype(jnp.float32)
        pw[l] = tall[...].astype(jnp.bfloat16)
        for b in range(bd_ref.shape[1]):
            pn[l, :, b * deep:(b + 1) * deep] = cbd_ref[bd_ref[l, b]]

    pl.semaphore_wait(barrier, par_count - 1 + ex_count // 2)

    for i in range(BANK_PIECES):
        span = pl.ds(i * piece_rows, piece_rows)
        for k in range(1, ex_count // 2):
            pltpu.make_async_remote_copy(
                bank_ref.at[span, :], banks.at[ex, i], bank_send.at[k, i], bank_recv.at[ex, i],
                device_id={"ex": lax.rem(ex + 2 * k, ex_count)}, device_id_type=MESH,
            ).start()
    for i in range(BANK_PIECES):
        span = pl.ds(i * piece_rows, piece_rows)
        pltpu.make_async_remote_copy(
            bank_ref.at[span, :], banks.at[ex, i], bank_send.at[0, i], bank_recv.at[ex, i],
            device_id={"ex": sibling}, device_id_type=MESH,
        ).start()

    def project(l, c):
        span = pl.ds(0, size)
        pltpu.make_async_copy(g1_ref.at[:, span], wide_s.at[l, c], in_sem.at[l, c, 0]).wait()
        pltpu.make_async_copy(x1_ref.at[span, :], narrow_s.at[l, c], in_sem.at[l, c, 1]).wait()
        first = jnp.dot(pw[l], wide_s[l, c], preferred_element_type=jnp.float32)
        second = lax.dot_general(
            pn[l], narrow_s[l, c], (((1,), (1,)), ((), ())), preferred_element_type=jnp.float32
        )
        return first, second

    def partial_copy(step, l, c):
        return pltpu.make_async_remote_copy(
            stage.at[step], recv.at[me, lax.rem(c, per)], send_sem.at[step], recv_sem.at[me, lax.rem(c, per)],
            device_id={"par": l * group + c // per}, device_id_type=MESH,
        )

    sent = 2 * chunks - per

    def send_step(step, carry):
        l, c = order(step)
        first, second = project(l, c)
        stage[step, :rank, :] = first.astype(jnp.bfloat16)
        stage[step, rank:, :] = second.astype(jnp.bfloat16)
        partial_copy(step, l, c).start()
        return carry

    lax.fori_loop(0, sent, send_step, 0)

    def keep_step(j, carry):
        first, second = project(layer, place * per + j)
        own[j, :rank, :] = first
        own[j, rank:, :] = second
        return carry

    lax.fori_loop(0, per, keep_step, 0)

    entry = lax.broadcasted_iota(jnp.int32, onehot.shape, 0)
    onehot[...] = (entry == qid_ref[...]).astype(jnp.float32).astype(jnp.bfloat16)
    lane = lax.broadcasted_iota(jnp.int32, (count_ex, size), 1)
    which = lax.broadcasted_iota(jnp.int32, (count_ex, size), 0)
    starts = jnp.zeros((count_ex, size), jnp.int32)
    ends = jnp.zeros((count_ex, size), jnp.int32)
    total = jnp.int32(0)
    for e in range(count_ex):
        starts = jnp.where(which == e, total, starts)
        total = total + len_ref[0, e]
        ends = jnp.where(which == e, total, ends)
    outer[...] = jnp.zeros_like(outer)

    def bank_forward(i):
        for k in range(1, ex_count // 2):
            source = lax.rem(ex + 2 * k, ex_count)
            pltpu.make_async_remote_copy(
                banks.at[source, i], banks.at[source, i], bank_send.at[k, i], bank_recv.at[source, i],
                device_id={"ex": source}, device_id_type=MESH,
            ).wait_recv()
            pltpu.make_async_remote_copy(
                banks.at[source, i], banks.at[source, i], fwd_send.at[k, i], fwd_recv.at[source, i],
                device_id={"ex": sibling}, device_id_type=MESH,
            ).start()

    def add_outer(c):
        token = lane + c * size
        member = ((token >= starts) & (token < ends)).astype(jnp.float32)
        slab = rows[c, pl.ds(pl.multiple_of(layer * rank + place * width, width), width), :].astype(jnp.float32)
        for a in range(width):
            weighted[a * count_ex:(a + 1) * count_ex, :] = (member * slab[a:a + 1, :]).astype(jnp.bfloat16)
        inside = rows[c, pl.ds(pl.multiple_of((1 - layer) * rank, rank), rank), :]
        twice[:rank, :] = inside
        twice[rank:, :] = inside
        outer[...] += lax.dot_general(
            weighted[...], twice[...], (((1,), (1,)), ((), ())), preferred_element_type=jnp.float32
        )

    def row_copy(k, j):
        c = place * per + j
        return pltpu.make_async_remote_copy(
            rows.at[c], rows.at[c], row_send.at[k, j], row_recv.at[c],
            device_id={"par": layer * group + lax.rem(place + k, group)}, device_id_type=MESH,
        )

    done = 0
    for j in range(per):
        acc = own[j]
        for k in range(1, par_count):
            source = lax.rem(me + k, par_count)
            pltpu.make_async_remote_copy(
                stage.at[0], recv.at[source, j], send_sem.at[0], recv_sem.at[source, j],
                device_id={"par": source}, device_id_type=MESH,
            ).wait_recv()
            acc = acc + recv[source, j].astype(jnp.float32)
        c = place * per + j
        rows[c] = acc.astype(jnp.bfloat16)
        for k in range(1, group):
            row_copy(k, j).start()
        goal = BANK_PIECES * (j + 1) // per
        for i in range(done, goal):
            bank_forward(i)
        done = goal
        add_outer(c)
    for k in range(1, group):
        for j in range(per):
            c = lax.rem(place + k, group) * per + j
            pltpu.make_async_remote_copy(
                rows.at[c], rows.at[c], row_send.at[k, j], row_recv.at[c],
                device_id={"par": layer * group + lax.rem(place + k, group)}, device_id_type=MESH,
            ).wait_recv()
            add_outer(c)

    upper = lax.broadcasted_iota(jnp.int32, (count_ex, 2 * rank), 1) >= rank
    for pair in range(width // 2):
        even = outer[2 * pair * count_ex:(2 * pair + 1) * count_ex, :]
        odd = outer[(2 * pair + 1) * count_ex:(2 * pair + 2) * count_ex, :]
        grads[:, 2 * rank * pair:2 * rank * (pair + 1)] = jnp.where(upper, odd, even).astype(jnp.bfloat16)

    for copy in local_bank:
        copy.wait()
    for i in range(BANK_PIECES):
        pltpu.make_async_remote_copy(
            banks.at[sibling, i], banks.at[sibling, i], bank_send.at[0, i], bank_recv.at[sibling, i],
            device_id={"ex": sibling}, device_id_type=MESH,
        ).wait_recv()
        for k in range(1, ex_count // 2):
            source = lax.rem(sibling + 2 * k, ex_count)
            pltpu.make_async_remote_copy(
                banks.at[source, i], banks.at[source, i], fwd_send.at[k, i], fwd_recv.at[source, i],
                device_id={"ex": sibling}, device_id_type=MESH,
            ).wait_recv()

    every = banks[...].reshape(onehot.shape[0], grads.shape[1])
    against = lax.dot_general(grads[...], every, (((1,), (1,)), ((), ())), preferred_element_type=jnp.float32)
    high_part = against.astype(jnp.bfloat16)
    low_part = (against - high_part.astype(jnp.float32)).astype(jnp.bfloat16)
    both = jnp.concatenate([high_part, low_part], axis=0)
    picked = jnp.dot(both, onehot[...], preferred_element_type=jnp.float32)
    picked = picked[:count_ex] + picked[count_ex:]
    share = part_s.shape[2]
    for d in range(par_count):
        part_s[d] = picked[:, d * share:(d + 1) * share]
    for k in range(1, par_count):
        target = lax.rem(me + k, par_count)
        pltpu.make_async_remote_copy(
            part_s.at[target], part_r.at[me], sc_send.at[k], sc_recv.at[me],
            device_id={"par": target}, device_id_type=MESH,
        ).start()
    result = part_s[me]
    for k in range(1, par_count):
        source = lax.rem(me + k, par_count)
        pltpu.make_async_remote_copy(
            part_s.at[source], part_r.at[source], sc_send.at[k], sc_recv.at[source],
            device_id={"par": source}, device_id_type=MESH,
        ).wait_recv()
        result = result + part_r[source]
    out_ref[...] = result

    def sent_step(step, carry):
        l, c = order(step)
        partial_copy(step, l, c).wait_send()
        return carry

    lax.fori_loop(0, sent, sent_step, 0)
    for k in range(1, group):
        for j in range(per):
            row_copy(k, j).wait_send()
    for i in range(BANK_PIECES):
        span = pl.ds(i * piece_rows, piece_rows)
        for k in range(ex_count // 2):
            pltpu.make_async_remote_copy(
                bank_ref.at[span, :], banks.at[ex, i], bank_send.at[k, i], bank_recv.at[ex, i],
                device_id={"ex": sibling}, device_id_type=MESH,
            ).wait_send()
        for k in range(1, ex_count // 2):
            source = lax.rem(ex + 2 * k, ex_count)
            pltpu.make_async_remote_copy(
                banks.at[source, i], banks.at[source, i], fwd_send.at[k, i], fwd_recv.at[source, i],
                device_id={"ex": sibling}, device_id_type=MESH,
            ).wait_send()
    for k in range(1, par_count):
        target = lax.rem(me + k, par_count)
        pltpu.make_async_remote_copy(
            part_s.at[target], part_r.at[me], sc_send.at[k], sc_recv.at[me],
            device_id={"par": target}, device_id_type=MESH,
        ).wait_send()


def on_device(x_in1, g_out1, x_in2, g_out2, codebook_d, codebook_f, blocks_d, blocks_f, lengths, bank, query_ids):
    par_count = lax.axis_size("par")
    ex_count = lax.axis_size("ex")
    tokens, slim = x_in1.shape
    broad = g_out1.shape[1]
    rank = codebook_d.shape[2]
    group = par_count // LAYERS
    chunks = group * max(1, 4 // group)
    per = chunks // group
    size = tokens // chunks
    count_ex = lengths.shape[1]
    width = rank // group
    entries, dims = bank.shape
    queries = query_ids.shape[0]
    share = queries // par_count
    half = ex_count // 2
    bf16, f32 = jnp.bfloat16, jnp.float32
    dma = pltpu.SemaphoreType.DMA
    hbm = pl.BlockSpec(memory_space=pl.ANY)
    vmem = pl.BlockSpec(memory_space=pltpu.VMEM)
    smem = pl.BlockSpec(memory_space=pltpu.SMEM)
    return pl.pallas_call(
        functools.partial(kernel, par_count, ex_count, chunks),
        out_shape=jax.ShapeDtypeStruct((count_ex, share), f32),
        in_specs=[hbm, hbm, hbm, hbm, vmem, vmem, smem, smem, smem, hbm, vmem],
        out_specs=vmem,
        scratch_shapes=[
            pltpu.VMEM((LAYERS, chunks, broad, size), bf16),
            pltpu.VMEM((LAYERS, chunks, size, slim), bf16),
            pltpu.VMEM((rank, broad), f32),
            pltpu.VMEM((LAYERS, rank, broad), bf16),
            pltpu.VMEM((LAYERS, rank, slim), bf16),
            pltpu.VMEM((2 * chunks - per, 2 * rank, size), bf16),
            pltpu.VMEM((par_count, per, 2 * rank, size), bf16),
            pltpu.VMEM((per, 2 * rank, size), f32),
            pltpu.VMEM((chunks, 2 * rank, size), bf16),
            pltpu.VMEM((2 * rank, size), bf16),
            pltpu.VMEM((width * count_ex, size), bf16),
            pltpu.VMEM((width * count_ex, 2 * rank), f32),
            pltpu.VMEM((count_ex, dims), bf16),
            pltpu.VMEM((ex_count, BANK_PIECES, entries // BANK_PIECES, dims), bf16),
            pltpu.VMEM((ex_count * entries, queries), bf16),
            pltpu.VMEM((par_count, count_ex, share), f32),
            pltpu.VMEM((par_count, count_ex, share), f32),
            dma((LAYERS, chunks, 2)),
            dma((2 * chunks - per,)),
            dma((par_count, per)),
            dma((group, per)),
            dma((chunks,)),
            dma((BANK_PIECES,)),
            dma((half, BANK_PIECES)),
            dma((ex_count, BANK_PIECES)),
            dma((half, BANK_PIECES)),
            dma((ex_count, BANK_PIECES)),
            dma((par_count,)),
            dma((par_count,)),
        ],
        compiler_params=pltpu.CompilerParams(
            collective_id=0, has_side_effects=True, vmem_limit_bytes=56 * 1024 * 1024
        ),
    )(
        x_in1, g_out1.T, x_in2.T, g_out2, codebook_d.transpose(0, 2, 1), codebook_f.transpose(0, 2, 1),
        blocks_d, blocks_f, lengths, bank,
        query_ids.reshape(1, queries),
    )


def solution(mesh):
    return jax.shard_map(
        on_device,
        mesh=mesh,
        in_specs=(
            P(("groups", "ex"), "par"),
            P(("groups", "ex"), "par"),
            P(("groups", "ex"), "par"),
            P(("groups", "ex"), "par"),
            P(),
            P(),
            P(None, "par"),
            P(None, "par"),
            P(("groups", "ex"), None),
            P("ex", "par"),
            P(),
        ),
        out_specs=P(("groups", "ex"), "par"),
        check_vma=False,
    )
```
